256 devices in a mesh: dp: 32 (over z, x), tensor: 8 (over y, core).
Axes of the slice: x: 4, y: 4, z: 8, core: 2. Of those that a mesh axis runs over, the one named last changes fastest.
Arguments:
- hidden: bfloat16 [1024, 53248], P('dp', 'tensor'), may hold values from -6 to 6
- down_matrix: bfloat16 [53248, 16384], P('tensor', 'dp'), may hold values from -0.02734375 to 0.02734375
- down_factor_levels: bfloat16 [32, 64, 53248], P('dp', None, 'tensor'), may hold values from -127 to 127
- hidden_level_scale: float32 [32, 53248], P('dp', 'tensor'), as said below
- adapter_up_factors: bfloat16 [32, 64, 16384], P(None, None, 'dp'), may hold values from -0.75 to 0.75
- adapter_per_row: int32 [1024, 1], replicated, may hold values from 0 to 31; in each aligned block of 32 rows (0 to 31, 32 to 63, ...) at most 2 rows name the same one
Outputs:
- mixed: bfloat16 [1024, 16384], P('tensor', 'dp')
The draws below stay inside these ranges and needn't reach their ends.
Inputs may be any that keep to these rules, and one draw needn't show every extreme that they name: `adapter_per_row`: in each aligned block of 32 rows (the rows of one index of dp) no adapter is named by more than 2 rows, a bound that some block reaches. `hidden_level_scale`: Positive.
All inputs are finite; a program needn't handle non-finite values.
Results may differ from the reference program's by a relative error of at most 0.0053.
Values may be sent and summed in bfloat16 or wider, within the bound.
No kernel may reach another device: no remote copies, remote signals or barrier semaphores. Data moves between devices by JAX's collectives and lax.ppermute only.
A program may use at most 64 MiB of HBM per device.

```python
import math
import jax
import jax.numpy as jnp
import numpy as np
from jax import lax

MODEL_WIDTH = 16384
FF = 53248
ADAPTER_RANK = 64
ROWS_DEV = 32
ROWS = 1024
ADAPTER_COUNT = 32
MOST = 2
N_DP = 32
N_TENSOR = 8


def draw_down_factor_levels(key, part):
    key = jax.random.fold_in(key, 11)
    return jax.random.randint(key, (ADAPTER_COUNT, ADAPTER_RANK, FF), -127, 128).astype(jnp.bfloat16)


def draw_hidden_level_scale(key, part):
    key = jax.random.fold_in(key, 23)
    spread_rows = jax.random.uniform(key, (ADAPTER_COUNT, FF), jnp.float32, math.log(0.3), math.log(3.0))
    return jnp.exp(spread_rows) / (73.0 * math.sqrt(FF))


def block_levels(own_key, dims, pieces, low, high):
    def one(position, shards_of):
        draws = jax.random.uniform(jax.random.fold_in(jax.random.fold_in(own_key, 6), position), (shards_of,), jnp.float32, low / len(pieces), high / len(pieces))
        return jnp.repeat(jnp.exp(draws), dims[position] // shards_of).reshape((-1,) + (1,) * (len(dims) - position - 1))

    loudness = one(*pieces[0])
    for cut in pieces[1:]:
        loudness = loudness * one(*cut)
    return loudness


def deal_out(stream_key, own, number, rows, count, top, limit, skew):
    sequence = jax.random.permutation(stream_key, count)
    heavy_load, common = shares(count, rows * top, limit, skew, True), shares(count, rows * top, limit, skew, False)
    places = jnp.arange(count)

    def named(tallies, turn):
        used = int((tallies > 0).sum())
        fixed = max(1, used // 4)
        passed = fixed + (places - fixed + turn * (used - fixed)) % max(1, count - fixed)
        return jnp.zeros((count,), jnp.int32).at[sequence[jnp.where(places < fixed, places, passed)]].set(jnp.asarray(tallies, jnp.int32))

    tallies = jnp.where(number % 4 == 0, named(heavy_load, number // 4), named(common, number - number // 4 - 1))
    mixed = jax.random.permutation(jax.random.fold_in(own, 3), count)
    source_of, sink = mixed[0:count // 2 * 2:2], mixed[1:count // 2 * 2:2]
    slack = jnp.minimum(tallies[source_of] - 1, limit - tallies[sink]) // 2
    slack = jnp.where((source_of == sequence[0]) | (sink == sequence[0]) | (tallies[sink] == 0), 0, jnp.maximum(slack, 0))
    passed = jax.random.randint(jax.random.fold_in(own, 4), (count // 2,), 0, 1 << 20) % (slack + 1)
    tallies = tallies.at[source_of].add(-passed).at[sink].add(passed)
    members = jnp.searchsorted(jnp.cumsum(tallies), jnp.arange(rows * top), side="right").astype(jnp.int32)
    listing = members.reshape(top, rows).T
    listing = listing[jax.random.permutation(jax.random.fold_in(own, 1), rows)]
    turn = jax.random.randint(jax.random.fold_in(own, 2), (rows, 1), 0, top)
    return jnp.take_along_axis(listing, (jnp.arange(top)[None, :] + turn) % top, axis=1)


def shares(count, total, limit, skew, full):
    weights = [(1 << 20) // math.isqrt(rank ** skew) + 1 for rank in range(1, count + 1)]
    largest = limit if full else min(limit, max(-(-total // count), total * weights[0] // sum(weights)))
    least = 1 if total - largest >= count - 1 else 0
    given, spare = [largest] + [least] * (count - 1), total - largest - least * (count - 1)
    while spare > 0:
        movable = [i for i in range(1, count) if given[i] < largest] or [i for i in range(1, count) if given[i] < limit]
        mass, remaining = sum([weights[i] for i in movable]), spare
        for i in movable:
            extra = min(limit - given[i], max(1, remaining * weights[i] // mass), spare)
            given[i] = given[i] + extra
            spare = spare - extra
    return np.array(given)


def scatter_about(rng, shape, width, most, shards=(), kind=jnp.bfloat16):
    array = width * jax.random.normal(rng, shape, jnp.float32)
    if shards:
        array = array * block_levels(rng, shape, shards, -0.22, 0.18)
    return jnp.clip(array, -most, most).astype(kind)


def setup_inputs(seed: int = 0) -> dict:
    key_list = jax.random.split(jax.random.key(seed), 7)
    hidden = scatter_about(key_list[0], (ROWS, FF), 1.0, 6.0, ((0, 32), (1, 8)))
    down_matrix = scatter_about(key_list[1], (FF, MODEL_WIDTH), FF ** -0.5, 0.02734375, ((0, 8), (1, 32)))
    down_factor_levels = draw_down_factor_levels(jax.random.fold_in(key_list[6], 71), 0)
    hidden_level_scale = draw_hidden_level_scale(jax.random.fold_in(key_list[6], 71), 0)
    adapter_up_factors = scatter_about(key_list[4], (ADAPTER_COUNT, ADAPTER_RANK, MODEL_WIDTH), ADAPTER_RANK ** -0.5, 0.75, ((2, 32),))
    adapter_per_row_keys = jax.random.split(jax.random.fold_in(key_list[5], 1), ROWS // ROWS_DEV)
    adapter_per_row_turns = jax.random.permutation(jax.random.fold_in(key_list[5], 3), ROWS // ROWS_DEV)
    adapter_per_row = jax.vmap(lambda own, number: deal_out(jax.random.fold_in(key_list[5], 2), own, number, ROWS_DEV, ADAPTER_COUNT, 1, MOST, 2))(adapter_per_row_keys, adapter_per_row_turns).reshape((ROWS, 1))
    return dict(hidden=hidden, down_matrix=down_matrix, down_factor_levels=down_factor_levels, hidden_level_scale=hidden_level_scale, adapter_up_factors=adapter_up_factors, adapter_per_row=adapter_per_row)


def reference(hidden, down_matrix, down_factor_levels, hidden_level_scale, adapter_up_factors, adapter_per_row):
    adapters = adapter_per_row[:, 0]
    base_projection = jnp.dot(hidden, down_matrix, preferred_element_type=jnp.float32)
    dense = (down_factor_levels.astype(jnp.float32) * hidden_level_scale[:, None, :]).astype(jnp.bfloat16)
    slice_len = FF // N_TENSOR
    blocks = hidden.reshape(N_DP, ROWS_DEV, N_TENSOR, slice_len)
    id_blocks = adapters.reshape(N_DP, ROWS_DEV)

    def shrink_block(pair):
        rows_block, ids_block = pair
        picked = dense[ids_block].astype(jnp.float32).reshape(ROWS_DEV, ADAPTER_RANK, N_TENSOR, slice_len)
        parts = jnp.einsum("rtf,rktf->rtk", rows_block.astype(jnp.float32), picked, precision=lax.Precision.HIGHEST)
        rounded = lax.optimization_barrier(parts.astype(jnp.bfloat16))
        return jnp.sum(rounded.astype(jnp.float32), axis=1)

    summed = lax.map(shrink_block, (blocks, id_blocks)).reshape(ROWS, ADAPTER_RANK)
    chosen = (adapters[:, None] == jnp.arange(ADAPTER_COUNT, dtype=jnp.int32)[None, :]).astype(jnp.float32)
    spread_rows = (chosen[:, :, None] * summed[:, None, :]).reshape(ROWS, ADAPTER_COUNT * ADAPTER_RANK)
    adapter_delta = jnp.dot(spread_rows, adapter_up_factors.astype(jnp.float32).reshape(ADAPTER_COUNT * ADAPTER_RANK, MODEL_WIDTH), precision=lax.Precision.HIGHEST, preferred_element_type=jnp.float32)
    return (base_projection + adapter_delta).astype(jnp.bfloat16)
```

```python
import functools

import jax
import jax.numpy as jnp
from jax import lax
from jax.experimental import pallas as pl
from jax.experimental.pallas import tpu as pltpu
from jax.sharding import Mesh, PartitionSpec as P

SIZES = {"z": 8, "x": 4}
BF16 = jnp.bfloat16
F32 = jnp.float32
I32 = jnp.int32
LANES = 128
NEAR, FAR = (1, 7, 2, 6), (3, 5, 4)
VMEM_LIMIT = 56 << 20


def turn(value, axis, by):
    size = SIZES[axis]
    pairs = [
        (i * 2 + c, (i + (by if c == 0 else -by)) % size * 2 + c)
        for i in range(size)
        for c in range(2)
    ]
    return lax.ppermute(value, (axis, "core"), pairs)


def after(value, *others):
    return lax.optimization_barrier((value, *others))[0]


def stack(*blocks):
    return jnp.concatenate(blocks, axis=0)


def dot(a, b, over=((1,), (0,))):
    return lax.dot_general(a, b, (over, ((), ())), preferred_element_type=F32)


def iota(shape, dim):
    return lax.broadcasted_iota(I32, shape, dim)


def plan_kernel(info, ids_ref, levels, scale, fill, pick, mask, dense, slot_of, slot_all):
    z, x, sign, t, me = (info[k] for k in range(5))
    rows = ids_ref.shape[1]
    rank = levels.shape[0]
    dense[...] = (levels[...].astype(F32) * scale[...]).astype(BF16)
    ids = ids_ref[...]
    lane, sub = iota(ids.shape, 1), iota(ids.shape, 0)
    place = jnp.zeros(ids.shape, I32)
    for q in range(rows):
        place += jnp.where((ids == ids[:, q : q + 1]) & (lane > q), 1, 0)
    slot_of[...] = jnp.where(ids == me, (sub >> 2) * 8 + (sub & 3) * 2 + place, -1)
    slot_all[...] = ids * 8 + (sub & 3) * 2 + place
    eye = iota((rows, rows), 0) == iota((rows, rows), 1)

    def column(row):
        return jnp.sum(jnp.where(eye, row, 0), axis=1, keepdims=True)

    def ones(where):
        return jnp.where(where, 1.0, 0.0).astype(BF16)

    for i in range(8):
        for j in range(4):
            source = ((z - sign * i) & 7) * 4 + ((x - sign * j) & 3)
            col = column(slot_of[pl.ds(source, 1), :])
            at = (i * 4 + j) * rows
            fill[at : at + rows, :] = ones(col == iota((rows, fill.shape[1]), 1))
    rank_bits = rank.bit_length() - 1
    for j in range(4):
        at = slice(j * rows, (j + 1) * rows)
        col = column(slot_all[pl.ds(t * 4 + j, 1), :])
        pick[at, :] = ones(col == iota((rows, pick.shape[1]), 1))
        col = column(ids_ref[pl.ds(t * 4 + j, 1), :])
        mask[at, :] = ones(col == (iota((rows, mask.shape[1]), 1) >> rank_bits))


def start(pairs, sems):
    copies = [pltpu.make_async_copy(src, dst, sems.at[k]) for k, (src, dst) in enumerate(pairs)]
    for copy in copies:
        copy.start()
    return copies


def wait(copies):
    for copy in copies:
        copy.wait()


def multiply(lhs, w, dense, acc):
    depth, n = w.shape
    half = depth // 2 if depth % 256 == 0 else depth
    for at in range(0, depth, half):
        at = slice(at, at + half)
        rows = lhs[:, at]
        base, shrink = dot(rows, w[at, :]), dot(rows, dense[:, at], ((1,), (1,)))
        if at.start:
            acc[:, :n] += base
            acc[:, n:] += shrink
        else:
            acc[:, :n], acc[:, n:] = base, shrink


def weight_copies(cut, weights, dense, w, d):
    first = [(weights.at[:cut], w.at[:cut]), (dense.at[:, :cut], d.at[:, :cut])]
    second = [(weights.at[cut:], w.at[cut:]), (dense.at[:, cut:], d.at[:, cut:])]
    return first, second


def both_products(cut, first, second, w, d, rows_a, rows_b, acc_a, acc_b, sems):
    copies = start(first + second, sems)
    wait(copies[: len(first)])
    multiply(rows_a, w.at[:cut], d.at[:, :cut], acc_a)
    wait(copies[len(first) :])
    multiply(rows_b, w.at[cut:], d.at[:, cut:], acc_b)


def finish(base, at, fill, block, parts):
    n = base.shape[1]
    both = stack(*parts)
    rows = both.shape[0]
    base[at : at + rows, :] = both[:, :n].astype(BF16)
    return dot(fill[block * rows : (block + 1) * rows, :], both[:, n:].astype(BF16), ((0,), (0,)))


def own_kernel(cut, *refs):
    own, (weights, dense, fill, base, slots), (w, d, rows_a, rows_b, acc_a, acc_b, sems) = (
        refs[:4], refs[4:9], refs[9:],
    )
    first, second = weight_copies(cut, weights, dense, w, d)
    rows = own[0].shape[0]
    for j in range(4):
        at = pl.ds(j * rows, rows)
        first.append((own[j].at[:, :cut], rows_a.at[at]))
        second.append((own[j].at[:, cut:], rows_b.at[at]))
    both_products(cut, first, second, w, d, rows_a, rows_b, acc_a, acc_b, sems)
    slots[...] = finish(base, 0, fill, 0, [acc_a[...] + acc_b[...]])


def near_kernel(cut, *refs):
    a, near, (weights, dense, acc_a, acc_b), (w, d, rows_a, rows_b, sems) = (
        refs[:4], refs[4:7], refs[7:11], refs[11:],
    )
    first, second = weight_copies(cut, weights, dense, w, d)
    for k in range(4):
        n = a[k].shape[0]
        first.append((a[k], rows_a.at[pl.ds(k * n, n)]))
        if k < 3:
            second.append((near[k], rows_b.at[pl.ds(k * n, n)]))
    both_products(cut, first, second, w, d, rows_a, rows_b, acc_a, acc_b, sems)


def far_kernel(cut, *refs):
    a, b, (weights, dense), (fill, near_a, near_b, earlier) = (
        refs[:2], refs[2:6], refs[6:8], refs[8:12],
    )
    base, acc_a, far_b, slots = refs[12:16]
    w, d, rows_a, rows_b, acc_b, sems = refs[16:]
    first, second = weight_copies(cut, weights, dense, w, d)
    at_b = 0
    for k in range(4):
        n, n_b = a[0].shape[0], b[k].shape[0]
        if k < 2:
            first.append((a[k], rows_a.at[pl.ds(k * n, n)]))
        second.append((b[k], rows_b.at[pl.ds(at_b, n_b)]))
        at_b += n_b
    both_products(cut, first, second, w, d, rows_a, rows_b, acc_a, acc_b, sems)
    rows = n // 4
    total = earlier[...]
    for k, i in enumerate(NEAR):
        parts = []
        for j in range(4):
            row = n * k + j * rows
            if j == 2:
                of_b = acc_b[k * rows : (k + 1) * rows, :]
            else:
                row_b = (j if j < 2 else 2) * n + k * rows
                of_b = near_b[row_b : row_b + rows, :]
            parts.append(near_a[row : row + rows, :] + of_b)
        total += finish(base, k * n, fill, i, parts)
    far_b[...] = acc_b[n:, :]
    slots[...] = total


def last_kernel(cut, info, a, far, weights, dense, fill, far_a, far_b, base_own, base_near, earlier, *refs):
    slots, out, (w, d, acc_a, acc_b, base, sems) = refs[0], refs[1:9], refs[9:]
    first, second = weight_copies(cut, weights, dense, w, d)
    both_products(cut, first, second, w, d, a, far, acc_a, acc_b, sems)
    n = a.shape[0]
    rows = n // 4
    total = earlier[...]
    base[:n, :] = base_own[...]
    for k, i in enumerate(NEAR):
        base[i * n : (i + 1) * n, :] = base_near[k * n : (k + 1) * n, :]
    for k, i in enumerate(FAR):
        parts = []
        for j in range(4):
            of_a = acc_a[j * rows : (j + 1) * rows, :] if k == 2 else None
            if k < 2:
                of_a = far_a[k * n + j * rows : k * n + (j + 1) * rows, :]
            if j == 2:
                of_b = acc_b[k * rows : (k + 1) * rows, :]
            else:
                row_b = ((j if j < 2 else 2) * 3 + k) * rows
                of_b = far_b[row_b : row_b + rows, :]
            parts.append(of_a + of_b)
        total += finish(base, i * n, fill, i, parts)
    rank = total.shape[1]
    slots[:, :rank], slots[:, rank:] = total, total
    z, _, sign, t, _ = (info[k] for k in range(5))
    for by, ref in enumerate(out):
        i = (sign * (z - t - by)) & 7
        ref[...] = base[pl.ds(pl.multiple_of(i * n, n), n), :]


def delta_kernel(slots, pick, mask, up, delta):
    mine = dot(pick[...], slots[...]).astype(BF16)
    spread = jnp.concatenate([mine] * (mask.shape[1] // LANES), axis=1) * mask[...]
    delta[...] = dot(spread, up[...])


def sum_kernel(info, delta, *refs):
    got, out, total = refs[:8], refs[8], refs[9]
    x, sign = info[1], info[2]
    rows = out.shape[0] // 4
    for j in range(4):
        at = slice(j * rows, (j + 1) * rows)
        other = slice((-j) % 4 * rows, ((-j) % 4 + 1) * rows)
        total[at, :] = sum(ref[other if by % 2 else at, :].astype(F32) for by, ref in enumerate(got))
    for k in range(4):
        j = (sign * (x - k)) & 3
        at = slice(k * rows, (k + 1) * rows)
        part = total[pl.ds(pl.multiple_of(j * rows, rows), rows), :]
        out[at, :] = (part + delta[at, :]).astype(BF16)


def local(kernel, out_shape, places, scratch=(), flops=1 << 20, name=None):
    vmem = pl.BlockSpec(memory_space=pltpu.VMEM)
    specs = {"s": pl.BlockSpec(memory_space=pltpu.SMEM), "v": vmem, "h": pl.BlockSpec(memory_space=pl.ANY)}
    return pl.pallas_call(
        kernel,
        out_shape=out_shape,
        in_specs=[specs[place] for place in places],
        out_specs=jax.tree.map(lambda _: vmem, out_shape),
        scratch_shapes=scratch,
        compiler_params=pltpu.CompilerParams(vmem_limit_bytes=VMEM_LIMIT),
        cost_estimate=pl.CostEstimate(flops=flops, bytes_accessed=4 << 20, transcendentals=0),
        name=name,
    )


def shards(hidden, down_matrix, levels, scale, up_factors, adapter_per_row):
    rows, width = hidden.shape
    rank = levels.shape[1]
    adapters = up_factors.shape[0]
    out_width = down_matrix.shape[1]
    z, x = lax.axis_index("z"), lax.axis_index("x")
    y, core = lax.axis_index("y"), lax.axis_index("core")
    me, t = z * 4 + x, y * 2 + core
    sign = 1 - 2 * core
    cut = width * 20 // 52 // 128 * 128
    levels = levels.reshape(rank, width)

    info = jnp.stack([z, x, sign, t, me]).astype(I32)
    fill, pick, mask, dense = local(
        plan_kernel,
        (
            jax.ShapeDtypeStruct((32 * rows, 64), BF16),
            jax.ShapeDtypeStruct((4 * rows, 8 * adapters), BF16),
            jax.ShapeDtypeStruct((4 * rows, adapters * rank), BF16),
            jax.ShapeDtypeStruct((rank, width), BF16),
        ),
        "svvv",
        [pltpu.VMEM((32, rows), I32), pltpu.VMEM((32, rows), I32)],
        name="plan",
    )(info, adapter_per_row.reshape(32, rows), levels, scale)

    n, wide = 4 * rows, out_width + rank
    block = jax.ShapeDtypeStruct((n, out_width), BF16)

    def sums(count):
        return jax.ShapeDtypeStruct((count * rows, wide), F32)

    def scratch(rows_a, rows_b, copies):
        rows_of = [((rows_a * rows, cut), BF16), ((rows_b * rows, width - cut), BF16)]
        return [
            pltpu.VMEM((width, out_width), BF16),
            pltpu.VMEM((rank, width), BF16),
            *(pltpu.VMEM(*shape) for shape in rows_of if shape[0][0]),
        ], [pltpu.SemaphoreType.DMA((copies,))]

    def acc(count):
        return pltpu.VMEM((count * rows, wide), F32)

    def cost(count):
        return 2 * count * rows * width * wide

    part_a, part_b = hidden[:, :cut], hidden[:, cut:]
    b = {0: part_b}
    b[1], b[7] = turn(part_b, "z", 1), turn(part_b, "z", -1)
    own_1, own_3 = turn(hidden, "x", 1), turn(hidden, "x", -1)
    b[2], b[6] = turn(b[1], "z", 1), turn(b[7], "z", -1)
    own_2 = turn(own_1, "x", 1)
    near_0 = stack(*(b[i] for i in NEAR))
    near_1, near_3 = turn(near_0, "x", 1), turn(near_0, "x", -1)
    b[3], b[5] = turn(b[2], "z", 1), turn(b[6], "z", -1)
    b[4] = turn(b[3], "z", 1)
    a = {0: after(stack(part_a, own_1[:, :cut], own_2[:, :cut], own_3[:, :cut]), b[3], b[5])}
    a[1], a[7] = turn(a[0], "z", 1), turn(a[0], "z", -1)
    head, tail = scratch(4, 4, 12)
    base_own, slots = local(
        functools.partial(own_kernel, cut),
        (block, jax.ShapeDtypeStruct((64, rank), F32)),
        "hhhhhhv",
        [*head, acc(4), acc(4), *tail],
        cost(4),
        "own",
    )(hidden, own_1, own_2, own_3, down_matrix, dense, fill)
    far_0 = after(stack(*(b[i] for i in FAR)), pick, mask)
    near_2 = turn(near_1, "x", 1)
    far_1, far_3 = turn(far_0, "x", 1), turn(far_0, "x", -1)
    a[2], a[6] = turn(after(a[1], base_own), "z", 1), turn(a[7], "z", -1)
    head, tail = scratch(16, 12, 11)
    near_a, near_b = local(
        functools.partial(near_kernel, cut),
        (sums(16), sums(12)),
        "hhhhhhhhh",
        [*head, *tail],
        cost(14),
        "near",
    )(*(a[i] for i in NEAR), near_0, near_1, near_3, down_matrix, dense)
    far_2 = turn(after(far_1, near_a, near_b), "x", 1)
    a[3], a[5] = turn(a[2], "z", 1), turn(a[6], "z", -1)
    a[4] = turn(a[3], "z", 1)
    head, tail = scratch(8, 13, 10)
    base_near, far_a, far_b, slots = local(
        functools.partial(far_kernel, cut),
        (
            jax.ShapeDtypeStruct((4 * n, out_width), BF16),
            sums(8),
            sums(9),
            jax.ShapeDtypeStruct((64, rank), F32),
        ),
        "hhhhhhhhvvvv",
        [*head, acc(13), *tail],
        cost(11),
        "far",
    )(a[3], a[5], near_2, far_0, far_1, far_3, down_matrix, dense, fill, near_a, near_b, slots)
    head, tail = scratch(0, 0, 4)
    slots, *blocks = local(
        functools.partial(last_kernel, cut),
        (jax.ShapeDtypeStruct((64, LANES), F32),) + (block,) * 8,
        "svvhhvvvvvv",
        [*head, acc(4), acc(3), pltpu.VMEM((8 * n, out_width), BF16), *tail],
        cost(4),
        "last",
    )(info, a[4], far_2, down_matrix, dense, fill, far_a, far_b, base_own, base_near, slots)

    slots = lax.all_to_all(slots, ("y", "core"), 0, 0, tiled=True)
    slots = jnp.sum(slots.reshape(8, 8, LANES), axis=0)
    slots = jnp.broadcast_to(slots[None], (adapters, 8, LANES)).reshape(adapters * 8, LANES)
    slots = lax.all_to_all(slots, ("z", "x"), 0, 0, tiled=True).astype(BF16)
    delta = local(
        delta_kernel,
        jax.ShapeDtypeStruct((n, out_width), F32),
        "vvvv",
        flops=2 * n * adapters * rank * out_width,
        name="delta",
    )(slots, pick, mask, up_factors.reshape(adapters * rank, out_width))

    got = [blocks[0]]
    for by in range(1, 8):
        pairs = [(i, (i + by) % 8) for i in range(8)]
        got.append(lax.ppermute(blocks[by], ("y", "core"), pairs))
    return local(
        sum_kernel, block, "s" + "v" * 9, [pltpu.VMEM((n, out_width), F32)], name="sum"
    )(info, delta, *got)


def solution(mesh):
    torus = Mesh(mesh.devices.reshape(8, 4, 4, 2), ("z", "x", "y", "core"))
    dp, tensor = ("z", "x"), ("y", "core")
    return jax.shard_map(
        shards,
        mesh=torus,
        in_specs=(
            P(dp, tensor),
            P(tensor, dp),
            P(dp, None, tensor),
            P(dp, tensor),
            P(None, None, dp),
            P(),
        ),
        out_specs=P(tensor, dp),
        check_vma=False,
    )
```

```python
import functools

import jax
import jax.numpy as jnp
from jax import lax
from jax.experimental import pallas as pl
from jax.experimental.pallas import tpu as pltpu
from jax.sharding import Mesh, PartitionSpec as P

SIZES = {"z": 8, "x": 4}
BF16 = jnp.bfloat16
F32 = jnp.float32
I32 = jnp.int32
LANES = 128
NEAR, FAR = (1, 7, 2, 6), (3, 5, 4)
VMEM_LIMIT = 16 << 20


def turn(value, axis, by):
    size = SIZES[axis]
    pairs = [
        (i * 2 + c, (i + (by if c == 0 else -by)) % size * 2 + c)
        for i in range(size)
        for c in range(2)
    ]
    return lax.ppermute(value, (axis, "core"), pairs)


def after(value, *others):
    return lax.optimization_barrier((value, *others))[0]


def stack(*blocks):
    return jnp.concatenate(blocks, axis=0)


def dot(a, b, over=((1,), (0,))):
    return lax.dot_general(a, b, (over, ((), ())), preferred_element_type=F32)


def iota(shape, dim):
    return lax.broadcasted_iota(I32, shape, dim)


def plan_kernel(info, ids_ref, levels, scale, fill, pick, mask, dense, slot_of, slot_all):
    z, x, sign, t, me = (info[k] for k in range(5))
    rows = ids_ref.shape[1]
    rank = levels.shape[0]
    dense[...] = (levels[...].astype(F32) * scale[...]).astype(BF16)
    ids = ids_ref[...]
    lane, sub = iota(ids.shape, 1), iota(ids.shape, 0)
    place = jnp.zeros(ids.shape, I32)
    for q in range(rows):
        place += jnp.where((ids == ids[:, q : q + 1]) & (lane > q), 1, 0)
    slot_of[...] = jnp.where(ids == me, (sub >> 2) * 8 + (sub & 3) * 2 + place, -1)
    slot_all[...] = ids * 8 + (sub & 3) * 2 + place
    eye = iota((rows, rows), 0) == iota((rows, rows), 1)

    def column(row):
        return jnp.sum(jnp.where(eye, row, 0), axis=1, keepdims=True)

    def ones(where):
        return jnp.where(where, 1.0, 0.0).astype(BF16)

    for i in range(8):
        for j in range(4):
            source = ((z - sign * i) & 7) * 4 + ((x - sign * j) & 3)
            col = column(slot_of[pl.ds(source, 1), :])
            at = (i * 4 + j) * rows
            fill[at : at + rows, :] = ones(col == iota((rows, fill.shape[1]), 1))
    rank_bits = rank.bit_length() - 1
    for j in range(4):
        at = slice(j * rows, (j + 1) * rows)
        col = column(slot_all[pl.ds(t * 4 + j, 1), :])
        pick[at, :] = ones(col == iota((rows, pick.shape[1]), 1))
        col = column(ids_ref[pl.ds(t * 4 + j, 1), :])
        mask[at, :] = ones(col == (iota((rows, mask.shape[1]), 1) >> rank_bits))


def start(pairs, sems):
    copies = [pltpu.make_async_copy(src, dst, sems.at[k]) for k, (src, dst) in enumerate(pairs)]
    for copy in copies:
        copy.start()
    return copies


def wait(copies):
    for copy in copies:
        copy.wait()


def multiply(lhs, w, dense, acc):
    depth, n = w.shape
    half = depth // 2 if depth % 256 == 0 else depth
    for at in range(0, depth, half):
        at = slice(at, at + half)
        rows = lhs[:, at]
        base, shrink = dot(rows, w[at, :]), dot(rows, dense[:, at], ((1,), (1,)))
        if at.start:
            acc[:, :n] += base
            acc[:, n:] += shrink
        else:
            acc[:, :n], acc[:, n:] = base, shrink


def both_products(cut, first, second, w, d, rows_a, rows_b, acc_a, acc_b, sems):
    copies = start(first + second, sems)
    wait(copies[: len(first)])
    multiply(rows_a, w.at[:cut], d.at[:, :cut], acc_a)
    wait(copies[len(first) :])
    multiply(rows_b, w.at[cut:], d.at[:, cut:], acc_b)


def finish(base, at, fill, block, parts):
    n = base.shape[1]
    both = stack(*parts)
    rows = both.shape[0]
    base[at : at + rows, :] = both[:, :n].astype(BF16)
    return dot(fill[block * rows : (block + 1) * rows, :], both[:, n:].astype(BF16), ((0,), (0,)))


def own_kernel(cut, *refs):
    own, (w, d, fill, base, slots), (rows_a, rows_b, acc_a, acc_b, sems) = (
        refs[:4], refs[4:9], refs[9:],
    )
    first, second = [], []
    rows = own[0].shape[0]
    for j in range(4):
        at = pl.ds(j * rows, rows)
        first.append((own[j].at[:, :cut], rows_a.at[at]))
        second.append((own[j].at[:, cut:], rows_b.at[at]))
    both_products(cut, first, second, w, d, rows_a, rows_b, acc_a, acc_b, sems)
    slots[...] = finish(base, 0, fill, 0, [acc_a[...] + acc_b[...]])


def near_kernel(cut, *refs):
    a, near, (w, d, acc_a, acc_b), (rows_a, rows_b, sems) = (
        refs[:4], refs[4:7], refs[7:11], refs[11:],
    )
    first, second = [], []
    for k in range(4):
        n = a[k].shape[0]
        first.append((a[k], rows_a.at[pl.ds(k * n, n)]))
        if k < 3:
            second.append((near[k], rows_b.at[pl.ds(k * n, n)]))
    both_products(cut, first, second, w, d, rows_a, rows_b, acc_a, acc_b, sems)


def far_kernel(cut, *refs):
    a, b, (w, d), (fill, near_a, near_b, earlier) = (
        refs[:2], refs[2:6], refs[6:8], refs[8:12],
    )
    base, acc_a, far_b, slots = refs[12:16]
    rows_a, rows_b, acc_b, sems = refs[16:]
    first, second = [], []
    at_b = 0
    for k in range(4):
        n, n_b = a[0].shape[0], b[k].shape[0]
        if k < 2:
            first.append((a[k], rows_a.at[pl.ds(k * n, n)]))
        second.append((b[k], rows_b.at[pl.ds(at_b, n_b)]))
        at_b += n_b
    both_products(cut, first, second, w, d, rows_a, rows_b, acc_a, acc_b, sems)
    rows = n // 4
    total = earlier[...]
    for k, i in enumerate(NEAR):
        parts = []
        for j in range(4):
            row = n * k + j * rows
            if j == 2:
                of_b = acc_b[k * rows : (k + 1) * rows, :]
            else:
                row_b = (j if j < 2 else 2) * n + k * rows
                of_b = near_b[row_b : row_b + rows, :]
            parts.append(near_a[row : row + rows, :] + of_b)
        total += finish(base, k * n, fill, i, parts)
    far_b[...] = acc_b[n:, :]
    slots[...] = total


def last_kernel(cut, info, a, far, w, d, fill, far_a, far_b, base_own, base_near, earlier,
                slots, keep, send, acc_a, acc_b, base, sems):
    multiply(a, w.at[:cut], d.at[:, :cut], acc_a)
    multiply(far, w.at[cut:], d.at[:, cut:], acc_b)
    n = a.shape[0]
    rows = n // 4
    total = earlier[...]
    base[:n, :] = base_own[...]
    for k, i in enumerate(NEAR):
        base[i * n : (i + 1) * n, :] = base_near[k * n : (k + 1) * n, :]
    for k, i in enumerate(FAR):
        parts = []
        for j in range(4):
            of_a = acc_a[j * rows : (j + 1) * rows, :] if k == 2 else None
            if k < 2:
                of_a = far_a[k * n + j * rows : k * n + (j + 1) * rows, :]
            if j == 2:
                of_b = acc_b[k * rows : (k + 1) * rows, :]
            else:
                row_b = ((j if j < 2 else 2) * 3 + k) * rows
                of_b = far_b[row_b : row_b + rows, :]
            parts.append(of_a + of_b)
        total += finish(base, i * n, fill, i, parts)
    rank = total.shape[1]
    slots[:, :rank], slots[:, rank:] = total, total
    z, sign, t = info[0], info[2], info[3]
    core = t & 1
    copies = []
    for by in range(4):
        for out, of in ((keep, core), (send, 1 - core)):
            i = (sign * (z - ((t - core + 2 * by) & 7) - of)) & 7
            copies.append((base.at[pl.ds(pl.multiple_of(i * n, n), n)], out.at[pl.ds(by * n, n)]))
    wait(start(copies, sems))


def swapped(ref, at, rows):
    return stack(*(ref[at + (-j) % 4 * rows : at + ((-j) % 4 + 1) * rows, :] for j in range(4)))


def pair_kernel(keep, got, *out):
    n = out[0].shape[0]
    for by, ref in enumerate(out):
        both = keep[by * n : (by + 1) * n, :].astype(F32) + swapped(got, by * n, n // 4).astype(F32)
        ref[...] = both.astype(ref.dtype)


def sum_kernel(info, slots, pick, mask, up, *refs):
    got, out, total = refs[:4], refs[4], refs[5]
    x, sign = info[1], info[2]
    rows = out.shape[0] // 4
    total[...] = sum(ref[...].astype(F32) for ref in got)
    mine = dot(pick[...], slots[...]).astype(BF16)
    spread = jnp.concatenate([mine] * (mask.shape[1] // LANES), axis=1) * mask[...]
    delta = dot(spread, up[...])
    for k in range(4):
        j = (sign * (x - k)) & 3
        part = total[pl.ds(pl.multiple_of(j * rows, rows), rows), :]
        at = slice(k * rows, (k + 1) * rows)
        out[at, :] = (part + delta[at, :]).astype(BF16)


def local(kernel, out_shape, places, scratch=(), flops=1 << 20, name=None, out="v"):
    vmem = pl.BlockSpec(memory_space=pltpu.VMEM)
    specs = {"s": pl.BlockSpec(memory_space=pltpu.SMEM), "v": vmem, "h": pl.BlockSpec(memory_space=pl.ANY)}
    return pl.pallas_call(
        kernel,
        out_shape=out_shape,
        in_specs=[specs[place] for place in places],
        out_specs=tuple(specs[p] for p in out) if len(out) > 1 else jax.tree.map(lambda _: vmem, out_shape),
        scratch_shapes=scratch,
        compiler_params=pltpu.CompilerParams(vmem_limit_bytes=VMEM_LIMIT),
        cost_estimate=pl.CostEstimate(flops=flops, bytes_accessed=4 << 20, transcendentals=0),
        name=name,
    )


def shards(hidden, down_matrix, levels, scale, up_factors, adapter_per_row):
    rows, width = hidden.shape
    rank = levels.shape[1]
    adapters = up_factors.shape[0]
    out_width = down_matrix.shape[1]
    z, x = lax.axis_index("z"), lax.axis_index("x")
    y, core = lax.axis_index("y"), lax.axis_index("core")
    me, t = z * 4 + x, y * 2 + core
    sign = 1 - 2 * core
    cut = width * 20 // 52 // 128 * 128
    levels = levels.reshape(rank, width)

    info = jnp.stack([z, x, sign, t, me]).astype(I32)
    fill, pick, mask, dense = local(
        plan_kernel,
        (
            jax.ShapeDtypeStruct((32 * rows, 64), BF16),
            jax.ShapeDtypeStruct((4 * rows, 8 * adapters), BF16),
            jax.ShapeDtypeStruct((4 * rows, adapters * rank), BF16),
            jax.ShapeDtypeStruct((rank, width), BF16),
        ),
        "svvv",
        [pltpu.VMEM((32, rows), I32), pltpu.VMEM((32, rows), I32)],
        name="plan",
    )(info, adapter_per_row.reshape(32, rows), levels, scale)

    n, wide = 4 * rows, out_width + rank
    block = jax.ShapeDtypeStruct((n, out_width), BF16)

    def sums(count):
        return jax.ShapeDtypeStruct((count * rows, wide), F32)

    def scratch(rows_a, rows_b, copies):
        rows_of = [((rows_a * rows, cut), BF16), ((rows_b * rows, width - cut), BF16)]
        return [
            *(pltpu.VMEM(*shape) for shape in rows_of if shape[0][0]),
        ], [pltpu.SemaphoreType.DMA((copies,))]

    def acc(count):
        return pltpu.VMEM((count * rows, wide), F32)

    def cost(count):
        return 2 * count * rows * width * wide

    part_a, part_b = hidden[:, :cut], hidden[:, cut:]
    b = {0: part_b}
    b[1], b[7] = turn(part_b, "z", 1), turn(part_b, "z", -1)
    own_1, own_3 = turn(hidden, "x", 1), turn(hidden, "x", -1)
    b[2], b[6] = turn(b[1], "z", 1), turn(b[7], "z", -1)
    own_2 = turn(own_1, "x", 1)
    near_0 = stack(*(b[i] for i in NEAR))
    near_1, near_3 = turn(near_0, "x", 1), turn(near_0, "x", -1)
    b[3], b[5] = turn(b[2], "z", 1), turn(b[6], "z", -1)
    b[4] = turn(b[3], "z", 1)
    a = {0: after(stack(part_a, own_1[:, :cut], own_2[:, :cut], own_3[:, :cut]), b[3], b[5])}
    a[1], a[7] = turn(a[0], "z", 1), turn(a[0], "z", -1)
    head, tail = scratch(4, 4, 12)
    base_own, slots = local(
        functools.partial(own_kernel, cut),
        (block, jax.ShapeDtypeStruct((64, rank), F32)),
        "hhhhvvv",
        [*head, acc(4), acc(4), *tail],
        cost(4),
        "own",
    )(hidden, own_1, own_2, own_3, down_matrix, dense, fill)
    far_0 = after(stack(*(b[i] for i in FAR)), pick, mask, near_1)
    near_2 = turn(near_1, "x", 1)
    far_1, far_3 = turn(far_0, "x", 1), turn(far_0, "x", -1)
    a[2], a[6] = turn(after(a[1], near_1), "z", 1), turn(after(a[7], near_3), "z", -1)
    head, tail = scratch(16, 12, 11)
    near_a, near_b = local(
        functools.partial(near_kernel, cut),
        (sums(16), sums(12)),
        "hhhhhhhvv",
        [*head, *tail],
        cost(14),
        "near",
    )(*(a[i] for i in NEAR), near_0, near_1, near_3, down_matrix, dense)
    far_2 = turn(far_1, "x", 1)
    a[3], a[5] = turn(after(a[2], base_own), "z", 1), turn(a[6], "z", -1)
    a[4] = turn(after(a[3], near_a, near_b), "z", 1)
    head, tail = scratch(8, 13, 10)
    base_near, far_a, far_b, slots = local(
        functools.partial(far_kernel, cut),
        (
            jax.ShapeDtypeStruct((4 * n, out_width), BF16),
            sums(8),
            sums(9),
            jax.ShapeDtypeStruct((64, rank), F32),
        ),
        "hhhhhhvvvvvv",
        [*head, acc(13), *tail],
        cost(11),
        "far",
    )(a[3], a[5], near_2, far_0, far_1, far_3, down_matrix, dense, fill, near_a, near_b, slots)
    four = jax.ShapeDtypeStruct((4 * n, out_width), BF16)
    slots, keep, send = local(
        functools.partial(last_kernel, cut),
        (jax.ShapeDtypeStruct((64, LANES), F32), four, four),
        "svvvvvvvvvv",
        [acc(4), acc(3), pltpu.VMEM((8 * n, out_width), BF16), pltpu.SemaphoreType.DMA((8,))],
        cost(4),
        "last",
        "vhh",
    )(info, a[4], far_2, down_matrix, dense, fill, far_a, far_b, base_own, base_near, slots)

    slots = lax.all_to_all(slots, ("y", "core"), 0, 0, tiled=True)
    slots = jnp.sum(slots.reshape(8, 8, LANES), axis=0)
    slots = jnp.broadcast_to(slots[None], (adapters, 8, LANES)).reshape(adapters * 8, LANES)
    slots = lax.all_to_all(slots, ("z", "x"), 0, 0, tiled=True).astype(BF16)

    given = lax.ppermute(send, "core", [(0, 1), (1, 0)])
    pairs = local(
        pair_kernel, (jax.ShapeDtypeStruct((n, out_width), F32), block, block, block), "vv", name="pair"
    )(keep, given)
    got = [pairs[0]]
    for by in range(1, 4):
        got.append(lax.ppermute(pairs[by], "y", [(i, (i + by) % 4) for i in range(4)]))
    return local(
        sum_kernel,
        block,
        "s" + "v" * 8,
        [pltpu.VMEM((n, out_width), F32)],
        2 * n * adapters * rank * out_width,
        "sum",
    )(info, slots, pick, mask, up_factors.reshape(adapters * rank, out_width), *got)


def solution(mesh):
    torus = Mesh(mesh.devices.reshape(8, 4, 4, 2), ("z", "x", "y", "core"))
    dp, tensor = ("z", "x"), ("y", "core")
    return jax.shard_map(
        shards,
        mesh=torus,
        in_specs=(
            P(dp, tensor),
            P(tensor, dp),
            P(dp, None, tensor),
            P(dp, tensor),
            P(None, None, dp),
            P(),
        ),
        out_specs=P(tensor, dp),
        check_vma=False,
    )
```

```python
import functools

import jax
import jax.numpy as jnp
from jax import lax
from jax.experimental import pallas as pl
from jax.experimental.pallas import tpu as pltpu
from jax.sharding import Mesh, PartitionSpec as P

SIZES = {"z": 8, "x": 4}
BF16 = jnp.bfloat16
F32 = jnp.float32
I32 = jnp.int32
LANES = 128
NEAR, FAR = (1, 7, 2, 6), (3, 5, 4)
DELTA_COST = 8_000_000_000
VMEM_LIMIT = 16 << 20


def turn(value, axis, by):
    size = SIZES[axis]
    pairs = [
        (i * 2 + c, (i + (by if c == 0 else -by)) % size * 2 + c)
        for i in range(size)
        for c in range(2)
    ]
    return lax.ppermute(value, (axis, "core"), pairs)


def after(value, *others):
    return lax.optimization_barrier((value, *others))[0]


def stack(*blocks):
    return jnp.concatenate(blocks, axis=0)


def dot(a, b, over=((1,), (0,))):
    return lax.dot_general(a, b, (over, ((), ())), preferred_element_type=F32)


def iota(shape, dim):
    return lax.broadcasted_iota(I32, shape, dim)


def plan_kernel(info, ids_ref, levels, scale, fill, mine, dense, slot_of, slot_all):
    z, x, sign, t, me = (info[k] for k in range(5))
    rows = ids_ref.shape[1]
    dense[...] = (levels[...].astype(F32) * scale[...]).astype(BF16)
    ids = ids_ref[...]
    lane, sub = iota(ids.shape, 1), iota(ids.shape, 0)
    place = jnp.zeros(ids.shape, I32)
    for q in range(rows):
        place += jnp.where((ids == ids[:, q : q + 1]) & (lane > q), 1, 0)
    slot_of[...] = jnp.where(ids == me, (sub >> 2) * 8 + (sub & 3) * 2 + place, -1)
    slot_all[...] = ids * 8 + (sub & 3) * 2 + place
    eye = iota((rows, rows), 0) == iota((rows, rows), 1)

    def column(row):
        return jnp.sum(jnp.where(eye, row, 0), axis=1, keepdims=True)

    def ones(where):
        return jnp.where(where, 1.0, 0.0).astype(BF16)

    for i in range(8):
        for j in range(4):
            source = ((z - sign * i) & 7) * 4 + ((x - sign * j) & 3)
            col = column(slot_of[pl.ds(source, 1), :])
            at = (i * 4 + j) * rows
            fill[at : at + rows, :] = ones(col == iota((rows, fill.shape[1]), 1))
    lane = iota((rows, LANES), 1)
    for j in range(4):
        slot, adapter = (column(ref[pl.ds(t * 4 + j, 1), :]) for ref in (slot_all, ids_ref))
        mine[j * rows : (j + 1) * rows, :] = jnp.where(lane == 0, slot, adapter)


def start(pairs, sems):
    copies = [pltpu.make_async_copy(src, dst, sems.at[k]) for k, (src, dst) in enumerate(pairs)]
    for copy in copies:
        copy.start()
    return copies


def wait(copies):
    for copy in copies:
        copy.wait()


def multiply(lhs, w, dense, acc):
    depth, n = w.shape
    half = depth // 2 if depth % 256 == 0 else depth
    for at in range(0, depth, half):
        at = slice(at, at + half)
        rows = lhs[:, at]
        for to, value in ((slice(0, n), w), (slice(n, None), dense)):
            if value is None:
                continue
            if value is w:
                part = dot(rows, w[at, :])
            else:
                part = dot(rows, dense[:, at], ((1,), (1,)))
            acc[:, to] = acc[:, to] + part if at.start else part


def both_products(cut, first, second, w, d, rows_a, rows_b, acc_a, acc_b, sems):
    copies = start(first + second, sems)
    wait(copies[: len(first)])
    multiply(rows_a, w.at[:cut], d.at[:, :cut], acc_a)
    wait(copies[len(first) :])
    multiply(rows_b, w.at[cut:], d.at[:, cut:], acc_b)


def finish(base, at, fill, block, parts):
    n = base.shape[1]
    both = stack(*parts)
    rows = both.shape[0]
    base[at : at + rows, :] = both[:, :n].astype(BF16)
    return dot(fill[block * rows : (block + 1) * rows, :], both[:, n:].astype(BF16), ((0,), (0,)))


def own_kernel(cut, *refs):
    own, (w, d, fill, base, slots), (rows_a, rows_b, acc_a, acc_b, sems) = (
        refs[:4], refs[4:9], refs[9:],
    )
    first, second = [], []
    rows = own[0].shape[0]
    for j in range(4):
        at = pl.ds(j * rows, rows)
        first.append((own[j].at[:, :cut], rows_a.at[at]))
        second.append((own[j].at[:, cut:], rows_b.at[at]))
    both_products(cut, first, second, w, d, rows_a, rows_b, acc_a, acc_b, sems)
    slots[...] = finish(base, 0, fill, 0, [acc_a[...] + acc_b[...]])


def near_kernel(cut, *refs):
    a, near, (w, d, acc_a, acc_b), (rows_a, rows_b, sems) = (
        refs[:4], refs[4:7], refs[7:11], refs[11:],
    )
    first, second = [], []
    for k in range(4):
        n = a[k].shape[0]
        first.append((a[k], rows_a.at[pl.ds(k * n, n)]))
        if k < 3:
            second.append((near[k], rows_b.at[pl.ds(k * n, n)]))
    both_products(cut, first, second, w, d, rows_a, rows_b, acc_a, acc_b, sems)


def far_kernel(cut, *refs):
    a, b, (w, d), (fill, near_a, near_b, earlier) = (
        refs[:2], refs[2:6], refs[6:8], refs[8:12],
    )
    base, acc_a, far_b, slots = refs[12:16]
    rows_a, rows_b, acc_b, sems = refs[16:]
    first, second = [], []
    at_b = 0
    for k in range(4):
        n, n_b = a[0].shape[0], b[k].shape[0]
        if k < 2:
            first.append((a[k], rows_a.at[pl.ds(k * n, n)]))
        second.append((b[k], rows_b.at[pl.ds(at_b, n_b)]))
        at_b += n_b
    both_products(cut, first, second, w, d, rows_a, rows_b, acc_a, acc_b, sems)
    rows = n // 4
    total = earlier[...]
    for k, i in enumerate(NEAR):
        parts = []
        for j in range(4):
            row = n * k + j * rows
            if j == 2:
                of_b = acc_b[k * rows : (k + 1) * rows, :]
            else:
                row_b = (j if j < 2 else 2) * n + k * rows
                of_b = near_b[row_b : row_b + rows, :]
            parts.append(near_a[row : row + rows, :] + of_b)
        total += finish(base, k * n, fill, i, parts)
    far_b[...] = acc_b[n:, :]
    slots[...] = total


def slots_kernel(cut, a, far, d, fill, far_a, far_b, earlier, slots):
    over = ((1,), (1,))
    last_a, last_b = dot(a[...], d[:, :cut], over), dot(far[...], d[:, cut:], over)
    n, rank = a.shape[0], d.shape[0]
    rows, width = n // 4, far_a.shape[1] - rank
    total = earlier[...]
    for k, i in enumerate(FAR):
        parts = []
        for j in range(4):
            if k == 2:
                of_a = last_a[j * rows : (j + 1) * rows, :]
            else:
                of_a = far_a[k * n + j * rows : k * n + (j + 1) * rows, width:]
            if j == 2:
                of_b = last_b[k * rows : (k + 1) * rows, :]
            else:
                row_b = ((j if j < 2 else 2) * 3 + k) * rows
                of_b = far_b[row_b : row_b + rows, width:]
            parts.append((of_a + of_b).astype(BF16))
        total += dot(fill[i * n : (i + 1) * n, :], stack(*parts), ((0,), (0,)))
    slots[:, :rank], slots[:, rank:] = total, total


def last_kernel(cut, info, a, far, w, far_a, far_b, base_own, base_near, keep, send, acc_a, acc_b, base, sems):
    multiply(a, w.at[:cut], None, acc_a)
    multiply(far, w.at[cut:], None, acc_b)
    n = a.shape[0]
    rows, width = n // 4, base.shape[1]
    base[:n, :] = base_own[...]
    for k, i in enumerate(NEAR):
        base[i * n : (i + 1) * n, :] = base_near[k * n : (k + 1) * n, :]
    for k, i in enumerate(FAR):
        parts = []
        for j in range(4):
            of_a = acc_a[j * rows : (j + 1) * rows, :] if k == 2 else None
            if k < 2:
                of_a = far_a[k * n + j * rows : k * n + (j + 1) * rows, :width]
            if j == 2:
                of_b = acc_b[k * rows : (k + 1) * rows, :]
            else:
                row_b = ((j if j < 2 else 2) * 3 + k) * rows
                of_b = far_b[row_b : row_b + rows, :width]
            parts.append(of_a + of_b)
        base[i * n : (i + 1) * n, :] = stack(*parts).astype(BF16)
    z, sign, t = info[0], info[2], info[3]
    core = t & 1
    copies = []
    for by in range(4):
        for out, of in ((keep, core), (send, 1 - core)):
            i = (sign * (z - ((t - core + 2 * by) & 7) - of)) & 7
            copies.append((base.at[pl.ds(pl.multiple_of(i * n, n), n)], out.at[pl.ds(by * n, n)]))
    wait(start(copies, sems))


def swapped(ref, at, rows):
    return stack(*(ref[at + (-j) % 4 * rows : at + ((-j) % 4 + 1) * rows, :] for j in range(4)))


def pair_kernel(keep, got, *out):
    n = out[0].shape[0]
    for by, ref in enumerate(out):
        both = keep[by * n : (by + 1) * n, :].astype(F32) + swapped(got, by * n, n // 4).astype(F32)
        ref[...] = both.astype(ref.dtype)


def load_kernel(source, out):
    out[...] = source[...]


def delta_kernel(rank, slots, mine, up, delta):
    slot, adapter = mine[:, :1], mine[:, 1:2]
    n = mine.shape[0]
    pick = jnp.where(slot == iota((n, slots.shape[0]), 1), 1.0, 0.0).astype(BF16)
    rows = dot(pick, slots[...]).astype(BF16)
    spread = jnp.concatenate([rows] * (up.shape[0] // LANES), axis=1)
    chosen = adapter == (iota(spread.shape, 1) >> (rank.bit_length() - 1))
    delta[...] = dot(jnp.where(chosen, spread, jnp.zeros((), BF16)), up[...])


def sum_kernel(info, delta, *refs):
    got, out, total = refs[:4], refs[4], refs[5]
    x, sign = info[1], info[2]
    rows = out.shape[0] // 4
    total[...] = sum(ref[...].astype(F32) for ref in got)
    for k in range(4):
        j = (sign * (x - k)) & 3
        part = total[pl.ds(pl.multiple_of(j * rows, rows), rows), :]
        at = slice(k * rows, (k + 1) * rows)
        out[at, :] = (part + delta[at, :]).astype(BF16)


def local(kernel, out_shape, places, scratch=(), flops=1 << 20, name=None, out="v"):
    vmem = pl.BlockSpec(memory_space=pltpu.VMEM)
    specs = {"s": pl.BlockSpec(memory_space=pltpu.SMEM), "v": vmem, "h": pl.BlockSpec(memory_space=pl.ANY)}
    return pl.pallas_call(
        kernel,
        out_shape=out_shape,
        in_specs=[specs[place] for place in places],
        out_specs=tuple(specs[p] for p in out) if len(out) > 1 else jax.tree.map(lambda _: vmem, out_shape),
        scratch_shapes=scratch,
        compiler_params=pltpu.CompilerParams(vmem_limit_bytes=VMEM_LIMIT),
        cost_estimate=pl.CostEstimate(flops=flops, bytes_accessed=4 << 20, transcendentals=0),
        name=name,
    )


def shards(hidden, down_matrix, levels, scale, up_factors, adapter_per_row):
    rows, width = hidden.shape
    rank = levels.shape[1]
    adapters = up_factors.shape[0]
    out_width = down_matrix.shape[1]
    z, x = lax.axis_index("z"), lax.axis_index("x")
    y, core = lax.axis_index("y"), lax.axis_index("core")
    me, t = z * 4 + x, y * 2 + core
    sign = 1 - 2 * core
    cut = width * 20 // 52 // 128 * 128
    levels = levels.reshape(rank, width)

    info = jnp.stack([z, x, sign, t, me]).astype(I32)
    fill, mine, dense = local(
        plan_kernel,
        (
            jax.ShapeDtypeStruct((32 * rows, 64), BF16),
            jax.ShapeDtypeStruct((4 * rows, LANES), I32),
            jax.ShapeDtypeStruct((rank, width), BF16),
        ),
        "svvv",
        [pltpu.VMEM((32, rows), I32), pltpu.VMEM((32, rows), I32)],
        name="plan",
    )(info, adapter_per_row.reshape(32, rows), levels, scale)

    n, wide = 4 * rows, out_width + rank
    block = jax.ShapeDtypeStruct((n, out_width), BF16)

    def sums(count):
        return jax.ShapeDtypeStruct((count * rows, wide), F32)

    def scratch(rows_a, rows_b, copies):
        rows_of = [((rows_a * rows, cut), BF16), ((rows_b * rows, width - cut), BF16)]
        return [
            *(pltpu.VMEM(*shape) for shape in rows_of if shape[0][0]),
        ], [pltpu.SemaphoreType.DMA((copies,))]

    def acc(count):
        return pltpu.VMEM((count * rows, wide), F32)

    def cost(count):
        return 2 * count * rows * width * wide

    part_a, part_b = hidden[:, :cut], hidden[:, cut:]
    b = {0: part_b}
    b[1], b[7] = turn(part_b, "z", 1), turn(part_b, "z", -1)
    own_1, own_3 = turn(hidden, "x", 1), turn(hidden, "x", -1)
    b[2], b[6] = turn(b[1], "z", 1), turn(b[7], "z", -1)
    own_2 = turn(own_1, "x", 1)
    near_0 = stack(*(b[i] for i in NEAR))
    near_1, near_3 = turn(near_0, "x", 1), turn(near_0, "x", -1)
    b[3], b[5] = turn(b[2], "z", 1), turn(b[6], "z", -1)
    b[4] = turn(b[3], "z", 1)
    a = {0: after(stack(part_a, own_1[:, :cut], own_2[:, :cut], own_3[:, :cut]), b[3], b[5])}
    a[1], a[7] = turn(a[0], "z", 1), turn(a[0], "z", -1)
    head, tail = scratch(4, 4, 12)
    base_own, slots = local(
        functools.partial(own_kernel, cut),
        (block, jax.ShapeDtypeStruct((64, rank), F32)),
        "hhhhvvv",
        [*head, acc(4), acc(4), *tail],
        cost(4),
        "own",
    )(hidden, own_1, own_2, own_3, down_matrix, dense, fill)
    far_0 = after(stack(*(b[i] for i in FAR)), mine, near_1)
    near_2 = turn(near_1, "x", 1)
    far_1, far_3 = turn(far_0, "x", 1), turn(far_0, "x", -1)
    a[2], a[6] = turn(after(a[1], near_1), "z", 1), turn(after(a[7], near_1), "z", -1)
    head, tail = scratch(16, 12, 11)
    near_a, near_b = local(
        functools.partial(near_kernel, cut),
        (sums(16), sums(12)),
        "hhhhhhhvv",
        [*head, *tail],
        cost(14),
        "near",
    )(*(a[i] for i in NEAR), near_0, near_1, near_3, down_matrix, dense)
    far_2 = turn(far_1, "x", 1)
    a[3], a[5] = turn(after(a[2], base_own), "z", 1), turn(a[6], "z", -1)
    a[4] = turn(after(a[3], near_a, near_b), "z", 1)
    head, tail = scratch(8, 13, 10)
    base_near, far_a, far_b, slots = local(
        functools.partial(far_kernel, cut),
        (
            jax.ShapeDtypeStruct((4 * n, out_width), BF16),
            sums(8),
            sums(9),
            jax.ShapeDtypeStruct((64, rank), F32),
        ),
        "hhhhhhvvvvvv",
        [*head, acc(13), *tail],
        cost(11),
        "far",
    )(a[3], a[5], near_2, far_0, far_1, far_3, down_matrix, dense, fill, near_a, near_b, slots)
    four = jax.ShapeDtypeStruct((4 * n, out_width), BF16)
    slots = local(
        functools.partial(slots_kernel, cut),
        jax.ShapeDtypeStruct((64, LANES), F32),
        "v" * 7,
        flops=2 * n * width * rank,
        name="slots",
    )(a[4], far_2, dense, fill, far_a, far_b, slots)
    keep, send = local(
        functools.partial(last_kernel, cut),
        (four, four),
        "svvvvvvv",
        [
            pltpu.VMEM((n, out_width), F32),
            pltpu.VMEM((3 * rows, out_width), F32),
            pltpu.VMEM((8 * n, out_width), BF16),
            pltpu.SemaphoreType.DMA((8,)),
        ],
        cost(4),
        "last",
        "hh",
    )(info, after(a[4], slots), far_2, down_matrix, far_a, far_b, base_own, base_near)

    slots = lax.all_to_all(slots, ("y", "core"), 0, 0, tiled=True)
    slots = jnp.sum(slots.reshape(8, 8, LANES), axis=0)
    slots = jnp.broadcast_to(slots[None], (adapters, 8, LANES)).reshape(adapters * 8, LANES)
    shared = slots
    slots = lax.all_to_all(slots, ("z", "x"), 0, 0, tiled=True).astype(BF16)

    given = lax.ppermute(send, "core", [(0, 1), (1, 0)])
    pairs = local(
        pair_kernel, (jax.ShapeDtypeStruct((n, out_width), F32), block, block, block), "vv", name="pair"
    )(keep, given)
    got = [pairs[0]]
    for by in range(1, 4):
        got.append(lax.ppermute(pairs[by], "y", [(i, (i + by) % 4) for i in range(4)]))
    up = up_factors.reshape(adapters * rank, out_width)
    up = local(load_kernel, jax.ShapeDtypeStruct(up.shape, BF16), "v", name="load")(after(up, shared))
    delta = local(
        functools.partial(delta_kernel, rank),
        jax.ShapeDtypeStruct((n, out_width), F32),
        "vvv",
        flops=DELTA_COST,
        name="delta",
    )(slots, mine, up)
    return local(
        sum_kernel, block, "s" + "v" * 5, [pltpu.VMEM((n, out_width), F32)], name="sum"
    )(info, delta, *got)


def solution(mesh):
    torus = Mesh(mesh.devices.reshape(8, 4, 4, 2), ("z", "x", "y", "core"))
    dp, tensor = ("z", "x"), ("y", "core")
    return jax.shard_map(
        shards,
        mesh=torus,
        in_specs=(
            P(dp, tensor),
            P(tensor, dp),
            P(dp, None, tensor),
            P(dp, tensor),
            P(None, None, dp),
            P(),
        ),
        out_specs=P(tensor, dp),
        check_vma=False,
    )
```

```python
import functools

import jax
import jax.numpy as jnp
from jax import lax
from jax.experimental import pallas as pl
from jax.experimental.pallas import tpu as pltpu
from jax.sharding import Mesh, PartitionSpec as P

SIZES = {"z": 8, "x": 4}
BF16 = jnp.bfloat16
F32 = jnp.float32
I32 = jnp.int32
LANES = 128
NEAR, FAR = (1, 7, 2, 6), (3, 5, 4)
DELTA_COST = 8_000_000_000
VMEM_LIMIT = 16 << 20


def turn(value, axis, by):
    size = SIZES[axis]
    pairs = [
        (i * 2 + c, (i + (by if c == 0 else -by)) % size * 2 + c)
        for i in range(size)
        for c in range(2)
    ]
    return lax.ppermute(value, (axis, "core"), pairs)


def after(value, *others):
    return lax.optimization_barrier((value, *others))[0]


def stack(*blocks):
    return jnp.concatenate(blocks, axis=0)


def dot(a, b, over=((1,), (0,))):
    return lax.dot_general(a, b, (over, ((), ())), preferred_element_type=F32)


def iota(shape, dim):
    return lax.broadcasted_iota(I32, shape, dim)


def plan_kernel(info, ids_ref, levels, scale, fill, mine, dense, slot_of, slot_all):
    z, x, sign, t, me = (info[k] for k in range(5))
    rows = ids_ref.shape[1]
    dense[...] = (levels[...].astype(F32) * scale[...]).astype(BF16)
    ids = ids_ref[...]
    lane, sub = iota(ids.shape, 1), iota(ids.shape, 0)
    place = jnp.zeros(ids.shape, I32)
    for q in range(rows):
        place += jnp.where((ids == ids[:, q : q + 1]) & (lane > q), 1, 0)
    slot_of[...] = jnp.where(ids == me, (sub >> 2) * 8 + (sub & 3) * 2 + place, -1)
    slot_all[...] = ids * 8 + (sub & 3) * 2 + place
    eye = iota((rows, rows), 0) == iota((rows, rows), 1)

    def column(row):
        return jnp.sum(jnp.where(eye, row, 0), axis=1, keepdims=True)

    def ones(where):
        return jnp.where(where, 1.0, 0.0).astype(BF16)

    for i in range(8):
        for j in range(4):
            source = ((z - sign * i) & 7) * 4 + ((x - sign * j) & 3)
            col = column(slot_of[pl.ds(source, 1), :])
            at = (i * 4 + j) * rows
            fill[at : at + rows, :] = ones(col == iota((rows, fill.shape[1]), 1))
    lane = iota((rows, LANES), 1)
    for j in range(4):
        slot, adapter = (column(ref[pl.ds(t * 4 + j, 1), :]) for ref in (slot_all, ids_ref))
        mine[j * rows : (j + 1) * rows, :] = jnp.where(lane == 0, slot, adapter)


def start(pairs, sems):
    copies = [pltpu.make_async_copy(src, dst, sems.at[k]) for k, (src, dst) in enumerate(pairs)]
    for copy in copies:
        copy.start()
    return copies


def wait(copies):
    for copy in copies:
        copy.wait()


def multiply(lhs, w, dense, acc):
    depth, n = w.shape
    half = depth // 2 if depth % 256 == 0 else depth
    for at in range(0, depth, half):
        at = slice(at, at + half)
        rows = lhs[:, at]
        for to, value in ((slice(0, n), w), (slice(n, None), dense)):
            if value is None:
                continue
            if value is w:
                part = dot(rows, w[at, :])
            else:
                part = dot(rows, dense[:, at], ((1,), (1,)))
            acc[:, to] = acc[:, to] + part if at.start else part


def both_products(cut, first, second, w, d, rows_a, rows_b, acc_a, acc_b, sems):
    copies = start(first + second, sems)
    wait(copies[: len(first)])
    multiply(rows_a, w.at[:cut], d.at[:, :cut], acc_a)
    wait(copies[len(first) :])
    multiply(rows_b, w.at[cut:], d.at[:, cut:], acc_b)


def finish(base, at, fill, block, parts):
    n = base.shape[1]
    both = stack(*parts)
    rows = both.shape[0]
    base[at : at + rows, :] = both[:, :n].astype(BF16)
    return dot(fill[block * rows : (block + 1) * rows, :], both[:, n:].astype(BF16), ((0,), (0,)))


def own_kernel(cut, *refs):
    own, (w, d, fill, base, slots), (rows_a, rows_b, acc_a, acc_b, sems) = (
        refs[:4], refs[4:9], refs[9:],
    )
    first, second = [], []
    rows = own[0].shape[0]
    for j in range(4):
        at = pl.ds(j * rows, rows)
        first.append((own[j].at[:, :cut], rows_a.at[at]))
        second.append((own[j].at[:, cut:], rows_b.at[at]))
    both_products(cut, first, second, w, d, rows_a, rows_b, acc_a, acc_b, sems)
    slots[...] = finish(base, 0, fill, 0, [acc_a[...] + acc_b[...]])


def near_kernel(cut, *refs):
    a, near, (w, d, acc_a, acc_b), (rows_a, rows_b, sems) = (
        refs[:4], refs[4:7], refs[7:11], refs[11:],
    )
    first, second = [], []
    for k in range(4):
        n = a[k].shape[0]
        first.append((a[k], rows_a.at[pl.ds(k * n, n)]))
        if k < 3:
            second.append((near[k], rows_b.at[pl.ds(k * n, n)]))
    both_products(cut, first, second, w, d, rows_a, rows_b, acc_a, acc_b, sems)


def far_kernel(cut, *refs):
    a, b, (w, d), (fill, near_a, near_b, earlier) = (
        refs[:2], refs[2:6], refs[6:8], refs[8:12],
    )
    base, acc_a, far_b, slots = refs[12:16]
    rows_a, rows_b, acc_b, sems = refs[16:]
    first, second = [], []
    at_b = 0
    for k in range(4):
        n, n_b = a[0].shape[0], b[k].shape[0]
        if k < 2:
            first.append((a[k], rows_a.at[pl.ds(k * n, n)]))
        second.append((b[k], rows_b.at[pl.ds(at_b, n_b)]))
        at_b += n_b
    both_products(cut, first, second, w, d, rows_a, rows_b, acc_a, acc_b, sems)
    rows = n // 4
    total = earlier[...]
    for k, i in enumerate(NEAR):
        parts = []
        for j in range(4):
            row = n * k + j * rows
            if j == 2:
                of_b = acc_b[k * rows : (k + 1) * rows, :]
            else:
                row_b = (j if j < 2 else 2) * n + k * rows
                of_b = near_b[row_b : row_b + rows, :]
            parts.append(near_a[row : row + rows, :] + of_b)
        total += finish(base, k * n, fill, i, parts)
    far_b[...] = acc_b[n:, :]
    slots[...] = total


def slots_kernel(cut, a, far, d, fill, far_a, far_b, earlier, slots):
    over = ((1,), (1,))
    last_a, last_b = dot(a[...], d[:, :cut], over), dot(far[...], d[:, cut:], over)
    n, rank = a.shape[0], d.shape[0]
    rows, width = n // 4, far_a.shape[1] - rank
    total = earlier[...]
    for k, i in enumerate(FAR):
        parts = []
        for j in range(4):
            if k == 2:
                of_a = last_a[j * rows : (j + 1) * rows, :]
            else:
                of_a = far_a[k * n + j * rows : k * n + (j + 1) * rows, width:]
            if j == 2:
                of_b = last_b[k * rows : (k + 1) * rows, :]
            else:
                row_b = ((j if j < 2 else 2) * 3 + k) * rows
                of_b = far_b[row_b : row_b + rows, width:]
            parts.append((of_a + of_b).astype(BF16))
        total += dot(fill[i * n : (i + 1) * n, :], stack(*parts), ((0,), (0,)))
    slots[:, :rank], slots[:, rank:] = total, total


def last_kernel(cut, info, a, far, weights, far_a, far_b, base_own, base_near, keep, send,
                acc_a, acc_b, base, w, sems, sems_w):
    edges = [cut * k // 4 for k in range(4)] + [cut + (w.shape[0] - cut) * k // 4 for k in range(5)]
    parts = [pl.ds(at, to - at) for at, to in zip(edges, edges[1:])]
    loads = start([(weights.at[at], w.at[at]) for at in parts], sems_w)
    wait(loads[:4])
    multiply(a, w.at[:cut], None, acc_a)
    wait(loads[4:])
    multiply(far, w.at[cut:], None, acc_b)
    n = a.shape[0]
    rows, width = n // 4, base.shape[1]
    base[:n, :] = base_own[...]
    for k, i in enumerate(NEAR):
        base[i * n : (i + 1) * n, :] = base_near[k * n : (k + 1) * n, :]
    for k, i in enumerate(FAR):
        parts = []
        for j in range(4):
            of_a = acc_a[j * rows : (j + 1) * rows, :] if k == 2 else None
            if k < 2:
                of_a = far_a[k * n + j * rows : k * n + (j + 1) * rows, :width]
            if j == 2:
                of_b = acc_b[k * rows : (k + 1) * rows, :]
            else:
                row_b = ((j if j < 2 else 2) * 3 + k) * rows
                of_b = far_b[row_b : row_b + rows, :width]
            parts.append(of_a + of_b)
        base[i * n : (i + 1) * n, :] = stack(*parts).astype(BF16)
    z, sign, t = info[0], info[2], info[3]
    core = t & 1
    copies = []
    for by in range(4):
        for out, of in ((keep, core), (send, 1 - core)):
            i = (sign * (z - ((t - core + 2 * by) & 7) - of)) & 7
            copies.append((base.at[pl.ds(pl.multiple_of(i * n, n), n)], out.at[pl.ds(by * n, n)]))
    wait(start(copies, sems))


def swapped(ref, at, rows):
    return stack(*(ref[at + (-j) % 4 * rows : at + ((-j) % 4 + 1) * rows, :] for j in range(4)))


def pair_kernel(keep, got, *out):
    n = out[0].shape[0]
    for by, ref in enumerate(out):
        both = keep[by * n : (by + 1) * n, :].astype(F32) + swapped(got, by * n, n // 4).astype(F32)
        ref[...] = both.astype(ref.dtype)


def delta_kernel(rank, slots, mine, up, delta):
    slot, adapter = mine[:, :1], mine[:, 1:2]
    n = mine.shape[0]
    pick = jnp.where(slot == iota((n, slots.shape[0]), 1), 1.0, 0.0).astype(BF16)
    rows = dot(pick, slots[...]).astype(BF16)
    spread = jnp.concatenate([rows] * (up.shape[0] // LANES), axis=1)
    chosen = adapter == (iota(spread.shape, 1) >> (rank.bit_length() - 1))
    delta[...] = dot(jnp.where(chosen, spread, jnp.zeros((), BF16)), up[...])


def sum_kernel(info, delta, *refs):
    got, out, total = refs[:4], refs[4], refs[5]
    x, sign = info[1], info[2]
    rows = out.shape[0] // 4
    total[...] = sum(ref[...].astype(F32) for ref in got)
    for k in range(4):
        j = (sign * (x - k)) & 3
        part = total[pl.ds(pl.multiple_of(j * rows, rows), rows), :]
        at = slice(k * rows, (k + 1) * rows)
        out[at, :] = (part + delta[at, :]).astype(BF16)


def local(kernel, out_shape, places, scratch=(), flops=1 << 20, name=None, out="v", limit=VMEM_LIMIT):
    vmem = pl.BlockSpec(memory_space=pltpu.VMEM)
    specs = {"s": pl.BlockSpec(memory_space=pltpu.SMEM), "v": vmem, "h": pl.BlockSpec(memory_space=pl.ANY)}
    return pl.pallas_call(
        kernel,
        out_shape=out_shape,
        in_specs=[specs[place] for place in places],
        out_specs=tuple(specs[p] for p in out) if len(out) > 1 else jax.tree.map(lambda _: vmem, out_shape),
        scratch_shapes=scratch,
        compiler_params=pltpu.CompilerParams(vmem_limit_bytes=limit),
        cost_estimate=pl.CostEstimate(flops=flops, bytes_accessed=4 << 20, transcendentals=0),
        name=name,
    )


def shards(hidden, down_matrix, levels, scale, up_factors, adapter_per_row):
    rows, width = hidden.shape
    rank = levels.shape[1]
    adapters = up_factors.shape[0]
    out_width = down_matrix.shape[1]
    z, x = lax.axis_index("z"), lax.axis_index("x")
    y, core = lax.axis_index("y"), lax.axis_index("core")
    me, t = z * 4 + x, y * 2 + core
    sign = 1 - 2 * core
    cut = width * 20 // 52 // 128 * 128
    levels = levels.reshape(rank, width)

    info = jnp.stack([z, x, sign, t, me]).astype(I32)
    fill, mine, dense = local(
        plan_kernel,
        (
            jax.ShapeDtypeStruct((32 * rows, 64), BF16),
            jax.ShapeDtypeStruct((4 * rows, LANES), I32),
            jax.ShapeDtypeStruct((rank, width), BF16),
        ),
        "svvv",
        [pltpu.VMEM((32, rows), I32), pltpu.VMEM((32, rows), I32)],
        name="plan",
    )(info, adapter_per_row.reshape(32, rows), levels, scale)

    n, wide = 4 * rows, out_width + rank
    block = jax.ShapeDtypeStruct((n, out_width), BF16)

    def sums(count):
        return jax.ShapeDtypeStruct((count * rows, wide), F32)

    def scratch(rows_a, rows_b, copies):
        rows_of = [((rows_a * rows, cut), BF16), ((rows_b * rows, width - cut), BF16)]
        return [
            *(pltpu.VMEM(*shape) for shape in rows_of if shape[0][0]),
        ], [pltpu.SemaphoreType.DMA((copies,))]

    def acc(count):
        return pltpu.VMEM((count * rows, wide), F32)

    def cost(count):
        return 2 * count * rows * width * wide

    part_a, part_b = hidden[:, :cut], hidden[:, cut:]
    b = {0: part_b}
    b[1], b[7] = turn(part_b, "z", 1), turn(part_b, "z", -1)
    own_1, own_3 = turn(hidden, "x", 1), turn(hidden, "x", -1)
    b[2], b[6] = turn(b[1], "z", 1), turn(b[7], "z", -1)
    own_2 = turn(own_1, "x", 1)
    near_0 = stack(*(b[i] for i in NEAR))
    near_1, near_3 = turn(near_0, "x", 1), turn(near_0, "x", -1)
    b[3], b[5] = turn(b[2], "z", 1), turn(b[6], "z", -1)
    b[4] = turn(b[3], "z", 1)
    a = {0: after(stack(part_a, own_1[:, :cut], own_2[:, :cut], own_3[:, :cut]), b[3], b[5])}
    a[1], a[7] = turn(a[0], "z", 1), turn(a[0], "z", -1)
    head, tail = scratch(4, 4, 12)
    base_own, slots = local(
        functools.partial(own_kernel, cut),
        (block, jax.ShapeDtypeStruct((64, rank), F32)),
        "hhhhvvv",
        [*head, acc(4), acc(4), *tail],
        cost(4),
        "own",
    )(hidden, own_1, own_2, own_3, down_matrix, dense, fill)
    far_0 = after(stack(*(b[i] for i in FAR)), mine, near_1)
    near_2 = turn(near_1, "x", 1)
    far_1, far_3 = turn(far_0, "x", 1), turn(far_0, "x", -1)
    a[2], a[6] = turn(after(a[1], near_1), "z", 1), turn(after(a[7], near_1), "z", -1)
    head, tail = scratch(16, 12, 11)
    near_a, near_b = local(
        functools.partial(near_kernel, cut),
        (sums(16), sums(12)),
        "hhhhhhhvv",
        [*head, *tail],
        cost(14),
        "near",
    )(*(a[i] for i in NEAR), near_0, near_1, near_3, down_matrix, dense)
    far_2 = turn(far_1, "x", 1)
    a[3], a[5] = turn(after(a[2], base_own), "z", 1), turn(a[6], "z", -1)
    a[4] = turn(after(a[3], near_a, near_b), "z", 1)
    head, tail = scratch(8, 13, 10)
    base_near, far_a, far_b, slots = local(
        functools.partial(far_kernel, cut),
        (
            jax.ShapeDtypeStruct((4 * n, out_width), BF16),
            sums(8),
            sums(9),
            jax.ShapeDtypeStruct((64, rank), F32),
        ),
        "hhhhhhvvvvvv",
        [*head, acc(13), *tail],
        cost(11),
        "far",
    )(a[3], a[5], near_2, far_0, far_1, far_3, down_matrix, dense, fill, near_a, near_b, slots)
    four = jax.ShapeDtypeStruct((4 * n, out_width), BF16)
    slots = local(
        functools.partial(slots_kernel, cut),
        jax.ShapeDtypeStruct((64, LANES), F32),
        "v" * 7,
        flops=2 * n * width * rank,
        name="slots",
    )(a[4], far_2, dense, fill, far_a, far_b, slots)
    keep, send = local(
        functools.partial(last_kernel, cut),
        (four, four),
        "svvhvvvv",
        [
            pltpu.VMEM((n, out_width), F32),
            pltpu.VMEM((3 * rows, out_width), F32),
            pltpu.VMEM((8 * n, out_width), BF16),
            pltpu.VMEM((width, out_width), BF16),
            pltpu.SemaphoreType.DMA((8,)),
            pltpu.SemaphoreType.DMA((8,)),
        ],
        cost(4),
        "last",
        "hh",
        56 << 20,
    )(info, after(a[4], slots), far_2, down_matrix, far_a, far_b, base_own, base_near)

    slots = lax.all_to_all(slots, ("y", "core"), 0, 0, tiled=True)
    parts = slots
    slots = jnp.sum(after(parts, send).reshape(8, 8, LANES), axis=0)
    slots = jnp.broadcast_to(slots[None], (adapters, 8, LANES)).reshape(adapters * 8, LANES)
    slots = lax.all_to_all(slots, ("z", "x"), 0, 0, tiled=True).astype(BF16)

    given = lax.ppermute(after(send, parts), "core", [(0, 1), (1, 0)])
    pairs = local(
        pair_kernel, (jax.ShapeDtypeStruct((n, out_width), F32), block, block, block), "vv", name="pair"
    )(keep, given)
    got = [pairs[0]]
    for by in range(1, 4):
        got.append(lax.ppermute(pairs[by], "y", [(i, (i + by) % 4) for i in range(4)]))
    up = up_factors.reshape(adapters * rank, out_width)
    delta = local(
        functools.partial(delta_kernel, rank),
        jax.ShapeDtypeStruct((n, out_width), F32),
        "vvv",
        flops=DELTA_COST,
        name="delta",
    )(slots, mine, up)
    return local(
        sum_kernel, block, "s" + "v" * 5, [pltpu.VMEM((n, out_width), F32)], name="sum"
    )(info, delta, *got)


def solution(mesh):
    torus = Mesh(mesh.devices.reshape(8, 4, 4, 2), ("z", "x", "y", "core"))
    dp, tensor = ("z", "x"), ("y", "core")
    return jax.shard_map(
        shards,
        mesh=torus,
        in_specs=(
            P(dp, tensor),
            P(tensor, dp),
            P(dp, None, tensor),
            P(dp, tensor),
            P(None, None, dp),
            P(),
        ),
        out_specs=P(tensor, dp),
        check_vma=False,
    )
```
